32 devices in a mesh: row: 4 (over y, x), col: 8 (over z, core).
Axes of the slice: x: 2, y: 2, z: 4, core: 2. Of those that a mesh axis runs over, the one named last changes fastest.
Arguments:
- x_block: bfloat16 [64, 8192], P(None, ('col', 'row')), may hold values from -6 to 6
- tiles: bfloat16 [768, 256, 256], P(('row', 'col')), may hold values from -0.078125 to 0.078125
- coords: int32 [768, 2], P(('row', 'col')), may hold values from 0 to 7, as said below
- counts: int32 [32], P(('row', 'col')), may hold values from 9 to 24, as said below
Outputs:
- basis: float32 [64, 8192], P(None, ('row', 'col'))
- factor: float32 [64, 64], replicated
The draws below stay inside these ranges and needn't reach their ends.
Inputs may be any that keep to these rules, and one draw needn't show every extreme that they name: `coords`: column 0 is a tile row below 8, column 1 a tile column below 4; at the device of place p = i * 8 + j, slot 0 names tile row j. `counts`: some device uses all 24 slots.
All inputs are finite; a program needn't handle non-finite values.
Results may differ from the reference program's by a relative error of at most 0.0003.
Values may be sent and summed in bfloat16 or wider, within the bound.
No kernel may reach another device: no remote copies, remote signals or barrier semaphores. Data moves between devices by JAX's collectives and lax.ppermute only.
A program may use at most 64 MiB of HBM per device.

```python
import jax
import jax.numpy as jnp
from jax import lax

COLS = 64
TILE = 256
KMAX = 24
N = 8192
PIECES = 32
PIECE_TILES = 1
ROW_TILES = 8
COL_TILES = 4
SLOTS = 768
N_COL = 8


def draw_coords(key, part):
    first_key, second_key = jax.random.split(key)
    tile_rows = jax.random.randint(first_key, (PIECES, KMAX), 0, ROW_TILES, dtype=jnp.int32)
    tile_cols = jax.random.randint(second_key, (PIECES, KMAX), 0, COL_TILES, dtype=jnp.int32)
    device = jnp.arange(PIECES, dtype=jnp.int32)[:, None]
    slot_index = jnp.arange(KMAX, dtype=jnp.int32)[None, :]
    column_place = device % (ROW_TILES // PIECE_TILES)
    own_rows = column_place * PIECE_TILES + slot_index
    tile_rows = jnp.where(slot_index < PIECE_TILES, own_rows, tile_rows)
    return jnp.stack([tile_rows, tile_cols], axis=-1).reshape(PIECES * KMAX, 2)


def draw_counts(key, part):
    first_key, second_key = jax.random.split(key)
    lowest = max(PIECE_TILES, 2 * KMAX // 5)
    values = jax.random.randint(first_key, (PIECES,), lowest, KMAX + 1, dtype=jnp.int32)
    busiest = jax.random.randint(second_key, (), 0, PIECES, dtype=jnp.int32)
    return values.at[busiest].set(KMAX)


def levels(stream_key, extent, cuts, least, high):
    def one(dim, blocks):
        draws = jax.random.uniform(jax.random.fold_in(jax.random.fold_in(stream_key, 6), dim), (blocks,), jnp.float32, least / len(cuts), high / len(cuts))
        return jnp.repeat(jnp.exp(draws), extent[dim] // blocks).reshape((-1,) + (1,) * (len(extent) - dim - 1))

    factor_of = one(*cuts[0])
    for cut in cuts[1:]:
        factor_of = factor_of * one(*cut)
    return factor_of


def gaussian(key, dims, spread, most, pieces=(), held_as=jnp.bfloat16):
    values = jax.random.normal(key, dims, jnp.float32) * spread
    if len(pieces) > 0:
        values = levels(key, dims, pieces, -0.22, 0.18) * values
    return jnp.clip(values, min=-most, max=most).astype(held_as)


def setup_inputs(seed: int = 0) -> dict:
    seeds = jax.random.split(jax.random.key(seed), 5)
    return {
        "x_block": gaussian(seeds[0], (COLS, N), 1.0, 6.0, ((1, 32),)),
        "tiles": gaussian(seeds[1], (SLOTS, TILE, TILE), (TILE * KMAX) ** -0.5, 0.078125, ((0, 32),)),
        "coords": draw_coords(jax.random.fold_in(seeds[4], 71), 0),
        "counts": draw_counts(jax.random.fold_in(seeds[4], 71), 0),
    }


def block_product(block_cols, slot_tiles, slot_coords, slot_count):
    vector_count = block_cols.shape[0]
    tile_size = slot_tiles.shape[1]
    shaped = block_cols.reshape(vector_count, COL_TILES, tile_size)
    picked = jnp.take(shaped, slot_coords[:, 1], axis=1).astype(jnp.float32)
    contrib = jnp.einsum('ckj,kij->kci', picked, slot_tiles.astype(jnp.float32), precision=lax.Precision.HIGHEST)
    live_slots = jnp.arange(KMAX, dtype=jnp.int32) < slot_count
    onehot = ((slot_coords[:, 0][None, :] == jnp.arange(ROW_TILES, dtype=jnp.int32)[:, None]) & live_slots[None, :]).astype(jnp.float32)
    summed = jnp.einsum('rk,kci->cri', onehot, contrib, precision=lax.Precision.HIGHEST)
    return summed.reshape(vector_count, ROW_TILES * tile_size)

def reference(x_block, tiles, coords, counts):
    vector_count = x_block.shape[0]
    block_rows = ROW_TILES * TILE
    block_width = COL_TILES * TILE
    tiles_all = tiles.reshape(PIECES, KMAX, TILE, TILE)
    coords_all = coords.reshape(PIECES, KMAX, 2)

    def accumulate(running, inputs):
        device, slot_tiles, slot_coords, slot_count = inputs
        block_row = device // N_COL
        block_col = device % N_COL
        block_cols = lax.dynamic_slice_in_dim(x_block, (block_col * block_width).astype(jnp.int32), block_width, 1)
        partial_rows = block_product(block_cols, slot_tiles, slot_coords, slot_count)
        start = (block_row * block_rows).astype(jnp.int32)
        before = lax.dynamic_slice_in_dim(running, start, block_rows, 1)
        running = lax.dynamic_update_slice_in_dim(running, before + partial_rows, start, 1)
        return (running, None)
    initial = jnp.zeros((vector_count, N), jnp.float32)
    devices_index = jnp.arange(PIECES, dtype=jnp.int32)
    y_full, _ = lax.scan(accumulate, initial, (devices_index, tiles_all, coords_all, counts))
    gram_total = jnp.dot(y_full.astype(jnp.float32), y_full.T.astype(jnp.float32), precision=lax.Precision.HIGHEST, preferred_element_type=jnp.float32) / N
    lower_factor = jnp.linalg.cholesky(gram_total)
    basis = jax.scipy.linalg.solve_triangular(lower_factor, y_full, lower=True)
    return (basis, lower_factor.T)
```

```python
import functools

import jax
import jax.numpy as jnp
from jax import lax
from jax.experimental import pallas as pl
from jax.experimental.pallas import tpu as pltpu
from jax.sharding import PartitionSpec as P

F32 = jnp.float32
VMEM = pl.BlockSpec(memory_space=pltpu.VMEM)
SMEM = pl.BlockSpec(memory_space=pltpu.SMEM)
EXACT = lax.Precision.HIGHEST
PANEL = 8


def swap(x, axis, bits):
    return lax.ppermute(x, axis, [(i, i ^ bits) for i in range(lax.axis_size(axis))])


def total(x, axis, low):
    size = lax.axis_size(axis)
    while low < size:
        masks = [low, 2 * low, 3 * low] if 2 * low < size else [low]
        parts = [swap(x, axis, mask) for mask in reversed(masks)]
        x = functools.reduce(jnp.add, parts, x)
        low *= 4
    return x


def product_kernel(blocks, select, tiles, *refs):
    pieces, (keep, send, x_all, rows) = refs[:blocks], refs[blocks:]
    for k in range(blocks):
        x_all[k] = pieces[k][...]
    rows[...] = jnp.zeros_like(rows)
    for s in range(tiles.shape[0]):
        rows[select[1, s]] += lax.dot_general(
            x_all[select[0, s]], tiles[s], (((1,), (1,)), ((), ())), preferred_element_type=F32
        )
    half = keep.shape[0]
    keep[...] = rows[:half]
    send[...] = rows[half : 2 * half]


def gram_kernel(scale, *refs):
    parts, (y_out, gram_out) = refs[:-2], refs[-2:]
    y = functools.reduce(jnp.add, [part[...] for part in parts])
    y_out[...] = y
    gram_out[...] = scale * lax.dot_general(
        y, y, (((1,), (1,)), ((), ())), precision=EXACT, preferred_element_type=F32
    )


def factor_kernel(y_ref, *refs):
    grams, (basis, factor) = refs[:-2], refs[-2:]
    gram = functools.reduce(jnp.add, [g[...] for g in grams])
    order = gram.shape[0]
    width = y_ref.shape[1]
    rest = jnp.concatenate([y_ref[...], gram], axis=1)
    lanes = 128
    sub = lax.broadcasted_iota(jnp.int32, (PANEL, 1), 0)
    col = lax.broadcasted_iota(jnp.int32, (PANEL, order), 1)
    for p in range(0, order, PANEL):
        live = order - p
        columns = [
            jnp.broadcast_to(rest[:, width + p + m : width + p + m + 1], (live, lanes))
            for m in range(PANEL)
        ]
        top = rest[:PANEL]
        lower = []
        done = jnp.zeros_like(top)
        for m in range(PANEL):
            inverse = lax.rsqrt(columns[m][m : m + 1])
            low = columns[m] * inverse
            lower.append(low)
            for n in range(m + 1, PANEL):
                columns[n] = columns[n] - low * low[n : n + 1]
            wide = inverse[:, :1]
            row = top[m : m + 1] * wide
            done = jnp.where(sub == m, row, done)
            if m + 1 < PANEL:
                top = top - low[:PANEL, :1] * row
        basis[p : p + PANEL, :] = done[:, :width]
        factor[p : p + PANEL, :] = jnp.where(col >= sub + p, done[:, width:], 0.0)
        if live > PANEL:
            rest = rest[PANEL:]
            for m in range(PANEL):
                rest = rest - lower[m][PANEL:, :1] * done[m : m + 1]


def local(x_block, tiles, coords, counts):
    vectors, width = x_block.shape
    slots = tiles.shape[0]
    n_row, n_col = lax.axis_size("row"), lax.axis_size("col")
    chips = n_col // 2
    me_row, me_col = lax.axis_index("row"), lax.axis_index("col")

    pieces = [x_block] + [swap(x_block, "row", k) for k in range(n_row - 1, 0, -1)][::-1]
    place = coords[:, 0] ^ me_col
    live = jnp.arange(slots, dtype=jnp.int32) < counts[0]
    place = jnp.where(live, (place & 1) * chips + (place >> 1), n_col)
    select = jnp.stack([coords[:, 1] ^ me_row, place])
    part = jax.ShapeDtypeStruct((chips, vectors, width), F32)
    keep, send = pl.pallas_call(
        functools.partial(product_kernel, n_row),
        out_shape=(part, part),
        in_specs=[SMEM] + [VMEM] * (1 + n_row),
        out_specs=(VMEM, VMEM),
        scratch_shapes=[
            pltpu.VMEM((n_row, vectors, width), x_block.dtype),
            pltpu.VMEM((n_col + 1, vectors, width), F32),
        ],
        name="product",
    )(select, tiles, *pieces)

    chip = keep + swap(send, "col", 1)
    parts = [chip[0]] + [swap(chip[k], "col", 2 * k) for k in range(chips - 1, 0, -1)]
    y, gram = pl.pallas_call(
        functools.partial(gram_kernel, 1.0 / (width * n_row * n_col)),
        out_shape=(
            jax.ShapeDtypeStruct((vectors, width), F32),
            jax.ShapeDtypeStruct((vectors, vectors), F32),
        ),
        in_specs=[VMEM] * chips,
        out_specs=(VMEM, VMEM),
        name="gram",
    )(*parts)
    gram = gram + swap(gram, "col", 1)
    gram = total(gram, "row", 1)
    gram = total(gram, "col", 2)
    return pl.pallas_call(
        factor_kernel,
        out_shape=(
            jax.ShapeDtypeStruct((vectors, width), F32),
            jax.ShapeDtypeStruct((vectors, vectors), F32),
        ),
        in_specs=[VMEM, VMEM],
        out_specs=(VMEM, VMEM),
        name="factor",
    )(y, gram)


def solution(mesh):
    placed = (
        P(None, ("col", "row")),
        P(("row", "col"), None, None),
        P(("row", "col"), None),
        P(("row", "col")),
    )
    return jax.shard_map(
        local, mesh=mesh, in_specs=placed, out_specs=(P(None, ("row", "col")), P()), check_vma=False
    )
```

```python
import functools

import jax
import jax.numpy as jnp
from jax import lax
from jax.experimental import pallas as pl
from jax.experimental.pallas import tpu as pltpu
from jax.sharding import PartitionSpec as P

F32 = jnp.float32
VMEM = pl.BlockSpec(memory_space=pltpu.VMEM)
SMEM = pl.BlockSpec(memory_space=pltpu.SMEM)
EXACT = lax.Precision.HIGHEST
PANEL = 16


def swap(x, axis, bits):
    return lax.ppermute(x, axis, [(i, i ^ bits) for i in range(lax.axis_size(axis))])


def total(x, axis, low):
    size = lax.axis_size(axis)
    while low < size:
        masks = [low, 2 * low, 3 * low] if 2 * low < size else [low]
        parts = [swap(x, axis, mask) for mask in masks]
        x = functools.reduce(jnp.add, parts, x)
        low *= 4
    return x


def select_kernel(coords, select):
    me_row, me_col = lax.axis_index("row"), lax.axis_index("col")
    n_col = lax.axis_size("col")
    apart = coords[0:1, :] ^ me_col
    place = (apart & 1) * (n_col // 2) + (apart >> 1)
    select[0:1, :] = place
    select[1:2, :] = coords[1:2, :] ^ me_row


def product_kernel(order, select, counts, tiles, *refs):
    pieces, (keep, send, x_all, rows) = refs[: len(order)], refs[len(order) :]
    for k, piece in zip(order, pieces):
        x_all[k] = piece[...]
    rows[...] = jnp.zeros_like(rows)
    for s in range(tiles.shape[0]):
        place = jnp.where(s < counts[0], select[0, s], rows.shape[0] - 1)
        rows[place] += lax.dot_general(
            x_all[select[1, s]], tiles[s], (((1,), (1,)), ((), ())), preferred_element_type=F32
        )
    half = keep.shape[0]
    keep[...] = rows[:half]
    send[...] = rows[half : 2 * half]


def gram_kernel(scale, *refs):
    parts, (y_out, gram_out) = refs[:-2], refs[-2:]
    y = functools.reduce(jnp.add, [part[...] for part in parts])
    y_out[...] = y
    half = y.shape[0] // 2
    for k in range(2):
        gram_out[:, k * 2 * half : (k + 1) * 2 * half] = scale * lax.dot_general(
            y[k * half : (k + 1) * half],
            y,
            (((1,), (1,)), ((), ())),
            precision=EXACT,
            preferred_element_type=F32,
        )


def factor_kernel(y_ref, *refs):
    grams, (basis, factor) = refs[:-2], refs[-2:]
    gram = functools.reduce(jnp.add, [g[...] for g in grams])
    order = y_ref.shape[0]
    gram = jnp.concatenate([gram[:, :order], gram[:, order:]], axis=0)
    width = y_ref.shape[1]
    rest = jnp.concatenate([y_ref[...], gram], axis=1)
    lanes = 128
    sub = lax.broadcasted_iota(jnp.int32, (PANEL, 1), 0)
    col = lax.broadcasted_iota(jnp.int32, (PANEL, order), 1)
    for p in range(0, order, PANEL):
        live = order - p
        columns = [
            jnp.broadcast_to(rest[:, width + p + m : width + p + m + 1], (live, lanes))
            for m in range(PANEL)
        ]
        top = rest[:PANEL]
        lower = []
        done = jnp.zeros_like(top)
        for m in range(PANEL):
            inverse = lax.rsqrt(columns[m][m : m + 1])
            low = columns[m] * inverse
            lower.append(low)
            for n in range(m + 1, PANEL):
                columns[n] = columns[n] - low * low[n : n + 1]
            wide = inverse[:, :1]
            row = top[m : m + 1] * wide
            done = jnp.where(sub == m, row, done)
            if m + 1 < PANEL:
                top = top - low[:PANEL, :1] * row
        basis[p : p + PANEL, :] = done[:, :width]
        factor[p : p + PANEL, :] = jnp.where(col >= sub + p, done[:, width:], 0.0)
        if live > PANEL:
            rest = rest[PANEL:]
            for m in range(PANEL):
                rest = rest - lower[m][PANEL:, :1] * done[m : m + 1]


def local(x_block, tiles, coords, counts):
    vectors, width = x_block.shape
    n_row, n_col = lax.axis_size("row"), lax.axis_size("col")
    chips = n_col // 2

    order = (*range(2, n_row), 1)
    pieces = [swap(x_block, "row", k) for k in order]
    select = pl.pallas_call(
        select_kernel,
        out_shape=jax.ShapeDtypeStruct(coords.shape[::-1], jnp.int32),
        in_specs=[VMEM],
        out_specs=VMEM,
        compiler_params=pltpu.CompilerParams(vmem_limit_bytes=1 << 20),
        cost_estimate=pl.CostEstimate(flops=4 * 10**9, bytes_accessed=0, transcendentals=0),
        name="select",
    )(coords.T)
    select, counts = lax.optimization_barrier((select, counts))
    part = jax.ShapeDtypeStruct((chips, vectors, width), F32)
    keep, send = pl.pallas_call(
        functools.partial(product_kernel, (0, *order)),
        out_shape=(part, part),
        in_specs=[SMEM, SMEM] + [VMEM] * (1 + n_row),
        out_specs=(VMEM, VMEM),
        scratch_shapes=[
            pltpu.VMEM((n_row, vectors, width), x_block.dtype),
            pltpu.VMEM((n_col + 1, vectors, width), F32),
        ],
        compiler_params=pltpu.CompilerParams(vmem_limit_bytes=12 << 20),
        name="product",
    )(select, counts, tiles, x_block, *pieces)

    chip = keep + swap(send, "col", 1)
    parts = [chip[0]] + [swap(chip[k], "col", 2 * k) for k in (1, *range(chips - 1, 1, -1))]
    y, gram = pl.pallas_call(
        functools.partial(gram_kernel, 1.0 / (width * n_row * n_col)),
        out_shape=(
            jax.ShapeDtypeStruct((vectors, width), F32),
            jax.ShapeDtypeStruct((vectors // 2, 2 * vectors), F32),
        ),
        in_specs=[VMEM] * chips,
        out_specs=(VMEM, VMEM),
        compiler_params=pltpu.CompilerParams(vmem_limit_bytes=4 << 20),
        name="gram",
    )(*parts)
    gram = gram + swap(gram, "col", 1)
    gram = total(gram, "row", 1)
    gram = total(gram, "col", 2)
    return pl.pallas_call(
        factor_kernel,
        out_shape=(
            jax.ShapeDtypeStruct((vectors, width), F32),
            jax.ShapeDtypeStruct((vectors, vectors), F32),
        ),
        in_specs=[VMEM, VMEM],
        out_specs=(VMEM, VMEM),
        compiler_params=pltpu.CompilerParams(vmem_limit_bytes=4 << 20),
        name="factor",
    )(y, gram)


def solution(mesh):
    placed = (
        P(None, ("col", "row")),
        P(("row", "col"), None, None),
        P(("row", "col"), None),
        P(("row", "col")),
    )
    return jax.shard_map(
        local, mesh=mesh, in_specs=placed, out_specs=(P(None, ("row", "col")), P()), check_vma=False
    )
```

```python
import functools

import jax
import jax.numpy as jnp
from jax import lax
from jax.experimental import pallas as pl
from jax.experimental.pallas import tpu as pltpu
from jax.sharding import PartitionSpec as P

F32 = jnp.float32
VMEM = pl.BlockSpec(memory_space=pltpu.VMEM)
SMEM = pl.BlockSpec(memory_space=pltpu.SMEM)
EXACT = lax.Precision.HIGHEST
PANEL = 16


def swap(x, row, col):
    n_row, n_col = lax.axis_size("row"), lax.axis_size("col")
    pairs = [
        (i * n_col + j, (i ^ row) * n_col + (j ^ col)) for i in range(n_row) for j in range(n_col)
    ]
    return lax.ppermute(x, ("row", "col"), pairs)


def rounds(axis):
    size, low = lax.axis_size(axis), 1 if axis == "row" else 2
    while low < size:
        masks = [low, 2 * low, 3 * low] if 2 * low < size else [low]
        yield [(0, mask | 1) if axis == "col" else (mask, 1) for mask in masks]
        low *= 4


def mark_kernel(out):
    out[...] = jnp.zeros_like(out)


def select_kernel(coords, mark, select):
    me_row, me_col = lax.axis_index("row"), lax.axis_index("col")
    n_col = lax.axis_size("col")
    apart = coords[0:1, :] ^ me_col
    place = (apart & 1) * (n_col // 2) + (apart >> 1)
    select[0:1, :] = place
    select[1:2, :] = coords[1:2, :] ^ me_row


def product_kernel(order, select, counts, tiles, *refs):
    pieces, (keep, send, x_all, rows) = refs[: len(order)], refs[len(order) :]
    for k, piece in zip(order, pieces):
        x_all[k] = piece[...]
    rows[...] = jnp.zeros_like(rows)
    for s in range(tiles.shape[0]):
        place = jnp.where(s < counts[0], select[0, s], rows.shape[0] - 1)
        rows[place] += lax.dot_general(
            x_all[select[1, s]], tiles[s], (((1,), (1,)), ((), ())), preferred_element_type=F32
        )
    half = keep.shape[0]
    keep[...] = rows[:half]
    send[...] = rows[half : 2 * half]


def gram_kernel(scale, *refs):
    parts, (y_out, gram_out) = refs[:-2], refs[-2:]
    y = functools.reduce(jnp.add, [part[...] for part in parts])
    y_out[...] = y
    half = y.shape[0] // 2
    for k in range(2):
        gram_out[:, k * 2 * half : (k + 1) * 2 * half] = scale * lax.dot_general(
            y[k * half : (k + 1) * half],
            y,
            (((1,), (1,)), ((), ())),
            precision=EXACT,
            preferred_element_type=F32,
        )


def factor_kernel(y_ref, *refs):
    grams, (basis, factor) = refs[:-2], refs[-2:]
    gram = functools.reduce(jnp.add, [g[...] for g in grams])
    order = y_ref.shape[0]
    gram = jnp.concatenate([gram[:, :order], gram[:, order:]], axis=0)
    width = y_ref.shape[1]
    rest = jnp.concatenate([y_ref[...], gram], axis=1)
    lanes = 128
    sub = lax.broadcasted_iota(jnp.int32, (PANEL, 1), 0)
    col = lax.broadcasted_iota(jnp.int32, (PANEL, order), 1)
    for p in range(0, order, PANEL):
        live = order - p
        columns = [
            jnp.broadcast_to(rest[:, width + p + m : width + p + m + 1], (live, lanes))
            for m in range(PANEL)
        ]
        top = rest[:PANEL]
        lower = []
        done = jnp.zeros_like(top)
        for m in range(PANEL):
            inverse = lax.rsqrt(columns[m][m : m + 1])
            low = columns[m] * inverse
            lower.append(low)
            for n in range(m + 1, PANEL):
                columns[n] = columns[n] - low * low[n : n + 1]
            wide = inverse[:, :1]
            row = top[m : m + 1] * wide
            done = jnp.where(sub == m, row, done)
            if m + 1 < PANEL:
                top = top - low[:PANEL, :1] * row
        basis[p : p + PANEL, :] = done[:, :width]
        factor[p : p + PANEL, :] = jnp.where(col >= sub + p, done[:, width:], 0.0)
        if live > PANEL:
            rest = rest[PANEL:]
            for m in range(PANEL):
                rest = rest - lower[m][PANEL:, :1] * done[m : m + 1]


def local(x_block, tiles, coords, counts):
    vectors, width = x_block.shape
    n_row, n_col = lax.axis_size("row"), lax.axis_size("col")
    chips = n_col // 2

    order = sorted(range(1, n_row), key=lambda k: (k != 3, k))
    mate = swap(x_block, 0, 1)
    pieces = [swap(mate, k, 1) if k == 1 else swap(x_block, k, 0) for k in order]
    mark = pl.pallas_call(
        mark_kernel,
        out_shape=jax.ShapeDtypeStruct((8, 128), F32),
        out_specs=VMEM,
        compiler_params=pltpu.CompilerParams(vmem_limit_bytes=1 << 20),
        cost_estimate=pl.CostEstimate(flops=4 * 10**9, bytes_accessed=0, transcendentals=0),
        name="mark",
    )()
    select = pl.pallas_call(
        select_kernel,
        out_shape=jax.ShapeDtypeStruct(coords.shape[::-1], jnp.int32),
        in_specs=[VMEM, VMEM],
        out_specs=VMEM,
        compiler_params=pltpu.CompilerParams(vmem_limit_bytes=1 << 20),
        name="select",
    )(coords.T, mark)
    select, counts = lax.optimization_barrier((select, counts))
    part = jax.ShapeDtypeStruct((chips, vectors, width), F32)
    keep, send = pl.pallas_call(
        functools.partial(product_kernel, (0, *order)),
        out_shape=(part, part),
        in_specs=[SMEM, SMEM] + [VMEM] * (1 + n_row),
        out_specs=(VMEM, VMEM),
        scratch_shapes=[
            pltpu.VMEM((n_row, vectors, width), x_block.dtype),
            pltpu.VMEM((n_col + 1, vectors, width), F32),
        ],
        compiler_params=pltpu.CompilerParams(vmem_limit_bytes=12 << 20),
        name="product",
    )(select, counts, tiles, x_block, *pieces)

    chip = keep + swap(send, 0, 1)
    far = sorted(range(1, chips), key=lambda k: (k != 2, k))
    parts = [chip[0]] + [swap(chip[k], 0, 2 * k) for k in far]
    y, gram = pl.pallas_call(
        functools.partial(gram_kernel, 1.0 / (width * n_row * n_col)),
        out_shape=(
            jax.ShapeDtypeStruct((vectors, width), F32),
            jax.ShapeDtypeStruct((vectors // 2, 2 * vectors), F32),
        ),
        in_specs=[VMEM] * chips,
        out_specs=(VMEM, VMEM),
        compiler_params=pltpu.CompilerParams(vmem_limit_bytes=4 << 20),
        name="gram",
    )(*parts)
    grams = [gram, swap(gram, 0, 1)]
    for masks in (*rounds("row"), *rounds("col")):
        gram = functools.reduce(jnp.add, grams)
        grams = [gram] + [swap(gram, row, col) for row, col in masks]
    return pl.pallas_call(
        factor_kernel,
        out_shape=(
            jax.ShapeDtypeStruct((vectors, width), F32),
            jax.ShapeDtypeStruct((vectors, vectors), F32),
        ),
        in_specs=[VMEM] * (1 + len(grams)),
        out_specs=(VMEM, VMEM),
        compiler_params=pltpu.CompilerParams(vmem_limit_bytes=4 << 20),
        name="factor",
    )(y, *grams)


def solution(mesh):
    placed = (
        P(None, ("col", "row")),
        P(("row", "col"), None, None),
        P(("row", "col"), None),
        P(("row", "col")),
    )
    return jax.shard_map(
        local, mesh=mesh, in_specs=placed, out_specs=(P(None, ("row", "col")), P()), check_vma=False
    )
```

```python
import functools

import jax
import jax.numpy as jnp
from jax import lax
from jax.experimental import pallas as pl
from jax.experimental.pallas import tpu as pltpu
from jax.sharding import PartitionSpec as P

F32 = jnp.float32
VMEM = pl.BlockSpec(memory_space=pltpu.VMEM)
SMEM = pl.BlockSpec(memory_space=pltpu.SMEM)
EXACT = lax.Precision.HIGHEST
PANEL = 16


def swap(x, row, col):
    n_row, n_col = lax.axis_size("row"), lax.axis_size("col")
    pairs = [
        (i * n_col + j, (i ^ row) * n_col + (j ^ col)) for i in range(n_row) for j in range(n_col)
    ]
    return lax.ppermute(x, ("row", "col"), pairs)


def rounds(axis):
    size, low = lax.axis_size(axis), 1 if axis == "row" else 2
    while low < size:
        masks = [low, 2 * low, 3 * low] if 2 * low < size else [low]
        yield [(0, mask | 1) if axis == "col" else (mask, 1) for mask in masks]
        low *= 4


def mark_kernel(out):
    out[...] = jnp.zeros_like(out)


def select_kernel(coords, counts, mark, select):
    me_row, me_col = lax.axis_index("row"), lax.axis_index("col")
    n_col = lax.axis_size("col")
    apart = coords[0:1, :] ^ me_col
    place = (apart & 1) * (n_col // 2) + (apart >> 1)
    slot = lax.broadcasted_iota(jnp.int32, apart.shape, 1)
    select[0:1, :] = jnp.where(slot < counts[0], place, n_col)
    select[1:2, :] = coords[1:2, :] ^ me_row


def turn_kernel(tiles, turned):
    for s in range(tiles.shape[0]):
        turned[s] = tiles[s].T


def product_kernel(order, select, turned, *refs):
    pieces, (keep, send, x_all, rows) = refs[: len(order)], refs[len(order) :]
    for k, piece in zip(order, pieces):
        x_all[k] = piece[...]
    rows[...] = jnp.zeros_like(rows)
    for s in range(turned.shape[0]):
        rows[select[0, s]] += jnp.dot(x_all[select[1, s]], turned[s], preferred_element_type=F32)
    half = keep.shape[0]
    keep[...] = rows[:half]
    send[...] = rows[half : 2 * half]


def gram_kernel(scale, *refs):
    parts, (y_out, gram_out) = refs[:-2], refs[-2:]
    y = functools.reduce(jnp.add, [part[...] for part in parts])
    y_out[...] = y
    half = y.shape[0] // 2
    for k in range(2):
        gram_out[:, k * 2 * half : (k + 1) * 2 * half] = scale * lax.dot_general(
            y[k * half : (k + 1) * half],
            y,
            (((1,), (1,)), ((), ())),
            precision=EXACT,
            preferred_element_type=F32,
        )


def factor_kernel(y_ref, *refs):
    grams, (basis, factor) = refs[:-2], refs[-2:]
    gram = functools.reduce(jnp.add, [g[...] for g in grams])
    order = y_ref.shape[0]
    gram = jnp.concatenate([gram[:, :order], gram[:, order:]], axis=0)
    width = y_ref.shape[1]
    rest = jnp.concatenate([y_ref[...], gram], axis=1)
    lanes = 128
    sub = lax.broadcasted_iota(jnp.int32, (PANEL, 1), 0)
    col = lax.broadcasted_iota(jnp.int32, (PANEL, order), 1)
    for p in range(0, order, PANEL):
        live = order - p
        columns = [
            jnp.broadcast_to(rest[:, width + p + m : width + p + m + 1], (live, lanes))
            for m in range(PANEL)
        ]
        top = rest[:PANEL]
        lower = []
        done = jnp.zeros_like(top)
        for m in range(PANEL):
            inverse = lax.rsqrt(columns[m][m : m + 1])
            low = columns[m] * inverse
            lower.append(low)
            for n in range(m + 1, PANEL):
                columns[n] = columns[n] - low * low[n : n + 1]
            wide = inverse[:, :1]
            row = top[m : m + 1] * wide
            done = jnp.where(sub == m, row, done)
            if m + 1 < PANEL:
                top = top - low[:PANEL, :1] * row
        basis[p : p + PANEL, :] = done[:, :width]
        factor[p : p + PANEL, :] = jnp.where(col >= sub + p, done[:, width:], 0.0)
        if live > PANEL:
            rest = rest[PANEL:]
            for m in range(PANEL):
                rest = rest - lower[m][PANEL:, :1] * done[m : m + 1]


def local(x_block, tiles, coords, counts):
    vectors, width = x_block.shape
    n_row, n_col = lax.axis_size("row"), lax.axis_size("col")
    chips = n_col // 2

    order = sorted(range(1, n_row), key=lambda k: (k != 3, k))
    mate = swap(x_block, 0, 1)
    pieces = [swap(mate, k, 1) if k == 1 else swap(x_block, k, 0) for k in order]
    mark = pl.pallas_call(
        mark_kernel,
        out_shape=jax.ShapeDtypeStruct((8, 128), F32),
        out_specs=VMEM,
        compiler_params=pltpu.CompilerParams(vmem_limit_bytes=1 << 20),
        cost_estimate=pl.CostEstimate(flops=4 * 10**9, bytes_accessed=0, transcendentals=0),
        name="mark",
    )()
    mark, counts = lax.optimization_barrier((mark, counts))
    select = pl.pallas_call(
        select_kernel,
        out_shape=jax.ShapeDtypeStruct(coords.shape[::-1], jnp.int32),
        in_specs=[VMEM, SMEM, VMEM],
        out_specs=VMEM,
        compiler_params=pltpu.CompilerParams(vmem_limit_bytes=1 << 20),
        name="select",
    )(coords.T, counts, mark)
    turned = pl.pallas_call(
        turn_kernel,
        out_shape=jax.ShapeDtypeStruct(tiles.shape[:1] + tiles.shape[:0:-1], tiles.dtype),
        in_specs=[VMEM],
        out_specs=VMEM,
        compiler_params=pltpu.CompilerParams(vmem_limit_bytes=8 << 20),
        cost_estimate=pl.CostEstimate(flops=10**9, bytes_accessed=0, transcendentals=0),
        name="turn",
    )(tiles)
    part = jax.ShapeDtypeStruct((chips, vectors, width), F32)
    keep, send = pl.pallas_call(
        functools.partial(product_kernel, (0, *order)),
        out_shape=(part, part),
        in_specs=[VMEM] * (2 + n_row),
        out_specs=(VMEM, VMEM),
        scratch_shapes=[
            pltpu.VMEM((n_row, vectors, width), x_block.dtype),
            pltpu.VMEM((n_col + 1, vectors, width), F32),
        ],
        compiler_params=pltpu.CompilerParams(vmem_limit_bytes=12 << 20),
        name="product",
    )(select, turned, x_block, *pieces)

    chip = keep + swap(send, 0, 1)
    far = sorted(range(1, chips), key=lambda k: (k != 2, k))
    parts = [chip[0]] + [swap(chip[k], 0, 2 * k) for k in far]
    y, gram = pl.pallas_call(
        functools.partial(gram_kernel, 1.0 / (width * n_row * n_col)),
        out_shape=(
            jax.ShapeDtypeStruct((vectors, width), F32),
            jax.ShapeDtypeStruct((vectors // 2, 2 * vectors), F32),
        ),
        in_specs=[VMEM] * chips,
        out_specs=(VMEM, VMEM),
        compiler_params=pltpu.CompilerParams(vmem_limit_bytes=4 << 20),
        name="gram",
    )(*parts)
    grams = [gram, swap(gram, 0, 1)]
    for masks in (*rounds("row"), *rounds("col")):
        gram = functools.reduce(jnp.add, grams)
        grams = [gram] + [swap(gram, row, col) for row, col in masks]
    return pl.pallas_call(
        factor_kernel,
        out_shape=(
            jax.ShapeDtypeStruct((vectors, width), F32),
            jax.ShapeDtypeStruct((vectors, vectors), F32),
        ),
        in_specs=[VMEM] * (1 + len(grams)),
        out_specs=(VMEM, VMEM),
        compiler_params=pltpu.CompilerParams(vmem_limit_bytes=4 << 20),
        name="factor",
    )(y, *grams)


def solution(mesh):
    placed = (
        P(None, ("col", "row")),
        P(("row", "col"), None, None),
        P(("row", "col"), None),
        P(("row", "col")),
    )
    return jax.shard_map(
        local, mesh=mesh, in_specs=placed, out_specs=(P(None, ("row", "col")), P()), check_vma=False
    )
```

```python
import functools

import jax
import jax.numpy as jnp
from jax import lax
from jax.experimental import pallas as pl
from jax.experimental.pallas import tpu as pltpu
from jax.sharding import PartitionSpec as P

F32 = jnp.float32
VMEM = pl.BlockSpec(memory_space=pltpu.VMEM)
SMEM = pl.BlockSpec(memory_space=pltpu.SMEM)
EXACT = lax.Precision.HIGHEST
PANEL = 16


def swap(x, row, col):
    n_row, n_col = lax.axis_size("row"), lax.axis_size("col")
    pairs = [
        (i * n_col + j, (i ^ row) * n_col + (j ^ col)) for i in range(n_row) for j in range(n_col)
    ]
    return lax.ppermute(x, ("row", "col"), pairs)


def rounds(axis):
    size, low = lax.axis_size(axis), 1 if axis == "row" else 2
    while low < size:
        masks = [low, 2 * low, 3 * low] if 2 * low < size else [low]
        yield [(0, mask | 1) if axis == "col" else (mask, 1) for mask in masks]
        low *= 4


def mark_kernel(out):
    out[...] = jnp.zeros_like(out)


def select_kernel(coords, counts, mark, select):
    me_row, me_col = lax.axis_index("row"), lax.axis_index("col")
    n_col = lax.axis_size("col")
    apart = coords[0:1, :] ^ me_col
    place = (apart & 1) * (n_col // 2) + (apart >> 1)
    slot = lax.broadcasted_iota(jnp.int32, apart.shape, 1)
    select[0:1, :] = jnp.where(slot < counts[0], place, n_col)
    select[1:2, :] = coords[1:2, :] ^ me_row


def turn_kernel(tiles, turned):
    for s in range(tiles.shape[0]):
        turned[s] = tiles[s].T


def product_kernel(order, select, turned, *refs):
    pieces, (keep, send, x_all, rows) = refs[: len(order)], refs[len(order) :]
    for k, piece in zip(order, pieces):
        x_all[k] = piece[...]
    rows[...] = jnp.zeros_like(rows)
    for s in range(turned.shape[0]):
        rows[select[0, s]] += jnp.dot(x_all[select[1, s]], turned[s], preferred_element_type=F32)
    half = keep.shape[0]
    keep[...] = rows[:half]
    send[...] = rows[half : 2 * half]


def gram_kernel(scale, *refs):
    parts, (y_out, gram_out) = refs[:-2], refs[-2:]
    y = functools.reduce(jnp.add, [part[...] for part in parts])
    y_out[...] = y
    half = y.shape[0] // 2
    for k in range(2):
        gram_out[:, k * 2 * half : (k + 1) * 2 * half] = scale * lax.dot_general(
            y[k * half : (k + 1) * half],
            y,
            (((1,), (1,)), ((), ())),
            precision=EXACT,
            preferred_element_type=F32,
        )


def hand_kernel(came, _, out):
    out[...] = came[...]


def sum_kernel(*refs):
    refs[-1][...] = functools.reduce(jnp.add, [ref[...] for ref in refs[:-1]])


def factor_kernel(y_ref, *refs):
    grams, (basis, factor) = refs[:-2], refs[-2:]
    gram = functools.reduce(jnp.add, [g[...] for g in grams])
    order = y_ref.shape[0]
    gram = jnp.concatenate([gram[:, :order], gram[:, order:]], axis=0)
    width = y_ref.shape[1]
    rest = jnp.concatenate([y_ref[...], gram], axis=1)
    lanes = 128
    sub = lax.broadcasted_iota(jnp.int32, (PANEL, 1), 0)
    col = lax.broadcasted_iota(jnp.int32, (PANEL, order), 1)
    for p in range(0, order, PANEL):
        live = order - p
        columns = [
            jnp.broadcast_to(rest[:, width + p + m : width + p + m + 1], (live, lanes))
            for m in range(PANEL)
        ]
        top = rest[:PANEL]
        lower = []
        done = jnp.zeros_like(top)
        for m in range(PANEL):
            inverse = lax.rsqrt(columns[m][m : m + 1])
            low = columns[m] * inverse
            lower.append(low)
            for n in range(m + 1, PANEL):
                columns[n] = columns[n] - low * low[n : n + 1]
            wide = inverse[:, :1]
            row = top[m : m + 1] * wide
            done = jnp.where(sub == m, row, done)
            if m + 1 < PANEL:
                top = top - low[:PANEL, :1] * row
        basis[p : p + PANEL, :] = done[:, :width]
        factor[p : p + PANEL, :] = jnp.where(col >= sub + p, done[:, width:], 0.0)
        if live > PANEL:
            rest = rest[PANEL:]
            for m in range(PANEL):
                rest = rest - lower[m][PANEL:, :1] * done[m : m + 1]


def local(x_block, tiles, coords, counts):
    vectors, width = x_block.shape
    n_row, n_col = lax.axis_size("row"), lax.axis_size("col")
    chips = n_col // 2

    order = sorted(range(1, n_row), key=lambda k: (k != 3, k))
    mate = swap(x_block, 0, 1)
    pieces = [swap(mate, k, 1) if k == 1 else swap(x_block, k, 0) for k in order]
    mark = pl.pallas_call(
        mark_kernel,
        out_shape=jax.ShapeDtypeStruct((8, 128), F32),
        out_specs=VMEM,
        compiler_params=pltpu.CompilerParams(vmem_limit_bytes=1 << 20),
        cost_estimate=pl.CostEstimate(flops=4 * 10**9, bytes_accessed=0, transcendentals=0),
        name="mark",
    )()
    mark, counts = lax.optimization_barrier((mark, counts))
    select = pl.pallas_call(
        select_kernel,
        out_shape=jax.ShapeDtypeStruct(coords.shape[::-1], jnp.int32),
        in_specs=[VMEM, SMEM, VMEM],
        out_specs=VMEM,
        compiler_params=pltpu.CompilerParams(vmem_limit_bytes=1 << 20),
        name="select",
    )(coords.T, counts, mark)
    turned = pl.pallas_call(
        turn_kernel,
        out_shape=jax.ShapeDtypeStruct(tiles.shape[:1] + tiles.shape[:0:-1], tiles.dtype),
        in_specs=[VMEM],
        out_specs=VMEM,
        compiler_params=pltpu.CompilerParams(vmem_limit_bytes=8 << 20),
        cost_estimate=pl.CostEstimate(flops=10**9, bytes_accessed=0, transcendentals=0),
        name="turn",
    )(tiles)
    part = jax.ShapeDtypeStruct((chips, vectors, width), F32)
    keep, send = pl.pallas_call(
        functools.partial(product_kernel, (0, *order)),
        out_shape=(part, part),
        in_specs=[VMEM] * (2 + n_row),
        out_specs=(VMEM, VMEM),
        scratch_shapes=[
            pltpu.VMEM((n_row, vectors, width), x_block.dtype),
            pltpu.VMEM((n_col + 1, vectors, width), F32),
        ],
        compiler_params=pltpu.CompilerParams(vmem_limit_bytes=12 << 20),
        name="product",
    )(select, turned, x_block, *pieces)

    chip = keep + swap(send, 0, 1)
    far = sorted(range(1, chips), key=lambda k: (k != 2, k))
    parts = [chip[0]] + [swap(chip[k], 0, 2 * k) for k in far]
    y, gram = pl.pallas_call(
        functools.partial(gram_kernel, 1.0 / (width * n_row * n_col)),
        out_shape=(
            jax.ShapeDtypeStruct((vectors, width), F32),
            jax.ShapeDtypeStruct((vectors // 2, 2 * vectors), F32),
        ),
        in_specs=[VMEM] * chips,
        out_specs=(VMEM, VMEM),
        compiler_params=pltpu.CompilerParams(vmem_limit_bytes=4 << 20),
        name="gram",
    )(*parts)
    small = jax.ShapeDtypeStruct(gram.shape, F32)
    far = swap(gram, 3, 1)
    gram = gram + swap(gram, 0, 1)
    near = [swap(gram, k, 1) for k in (1, 2)]
    far = pl.pallas_call(
        hand_kernel,
        out_shape=small,
        in_specs=[VMEM] * 2,
        out_specs=VMEM,
        compiler_params=pltpu.CompilerParams(vmem_limit_bytes=1 << 20),
        name="hand",
    )(far, gram)
    fix = swap(far, 0, 1)
    grams = [fix, far, gram] + near
    for masks in (*list(rounds("row"))[1:], *rounds("col")):
        gram = pl.pallas_call(
            sum_kernel,
            out_shape=small,
            in_specs=[VMEM] * len(grams),
            out_specs=VMEM,
            compiler_params=pltpu.CompilerParams(vmem_limit_bytes=1 << 20),
            name="sum",
        )(*grams)
        grams = [gram] + [swap(gram, row, col) for row, col in masks]
    return pl.pallas_call(
        factor_kernel,
        out_shape=(
            jax.ShapeDtypeStruct((vectors, width), F32),
            jax.ShapeDtypeStruct((vectors, vectors), F32),
        ),
        in_specs=[VMEM] * (1 + len(grams)),
        out_specs=(VMEM, VMEM),
        compiler_params=pltpu.CompilerParams(vmem_limit_bytes=4 << 20),
        name="factor",
    )(y, *grams)


def solution(mesh):
    placed = (
        P(None, ("col", "row")),
        P(("row", "col"), None, None),
        P(("row", "col"), None),
        P(("row", "col")),
    )
    return jax.shard_map(
        local, mesh=mesh, in_specs=placed, out_specs=(P(None, ("row", "col")), P()), check_vma=False
    )
```

```python
import functools

import jax
import jax.numpy as jnp
from jax import lax
from jax.experimental import pallas as pl
from jax.experimental.pallas import tpu as pltpu
from jax.sharding import PartitionSpec as P

F32 = jnp.float32
VMEM = pl.BlockSpec(memory_space=pltpu.VMEM)
SMEM = pl.BlockSpec(memory_space=pltpu.SMEM)
EXACT = lax.Precision.HIGHEST
PANEL = 16


def swap(x, row, col):
    n_row, n_col = lax.axis_size("row"), lax.axis_size("col")
    pairs = [
        (i * n_col + j, (i ^ row) * n_col + (j ^ col)) for i in range(n_row) for j in range(n_col)
    ]
    return lax.ppermute(x, ("row", "col"), pairs)


def split_swap(x, first, second):
    n_col = lax.axis_size("col")
    return lax.ppermute(x, "col", [(j, j ^ (second if j & 1 else first)) for j in range(n_col)])


def rounds(axis):
    size, low = lax.axis_size(axis), 1 if axis == "row" else 2
    while low < size:
        masks = [low, 2 * low, 3 * low] if 2 * low < size else [low]
        yield [(0, mask | 1) if axis == "col" else (mask, 1) for mask in masks]
        low *= 4


def mark_kernel(out):
    out[...] = jnp.zeros_like(out)


def select_kernel(coords, counts, mark, select):
    me_row, me_col = lax.axis_index("row"), lax.axis_index("col")
    n_col = lax.axis_size("col")
    apart = coords[0:1, :] ^ me_col
    place = (apart & 1) * (n_col // 2) + (apart >> 1)
    slot = lax.broadcasted_iota(jnp.int32, apart.shape, 1)
    select[0:1, :] = jnp.where(slot < counts[0], place, n_col)
    select[1:2, :] = coords[1:2, :] ^ me_row


def turn_kernel(tiles, turned):
    for s in range(tiles.shape[0]):
        turned[s] = tiles[s].T


def product_kernel(order, select, turned, *refs):
    pieces, (keep, send, x_all, rows) = refs[: len(order)], refs[len(order) :]
    for k, piece in zip(order, pieces):
        x_all[k] = piece[...]
    rows[...] = jnp.zeros_like(rows)
    for s in range(turned.shape[0]):
        rows[select[0, s]] += jnp.dot(x_all[select[1, s]], turned[s], preferred_element_type=F32)
    half = keep.shape[0]
    keep[...] = rows[:half]
    send[...] = rows[half : 2 * half]


def gram_kernel(scale, *refs):
    parts, (y_out, gram_out) = refs[:-2], refs[-2:]
    y = functools.reduce(jnp.add, [part[...] for part in parts])
    y_out[...] = y
    half = y.shape[0] // 2
    for k in range(2):
        gram_out[:, k * 2 * half : (k + 1) * 2 * half] = scale * lax.dot_general(
            y[k * half : (k + 1) * half],
            y,
            (((1,), (1,)), ((), ())),
            precision=EXACT,
            preferred_element_type=F32,
        )


def hand_kernel(came, _, out):
    out[...] = came[...]


def sum_kernel(*refs):
    refs[-1][...] = functools.reduce(jnp.add, [ref[...] for ref in refs[:-1]])


def factor_kernel(y_ref, *refs):
    grams, (basis, factor) = refs[:-2], refs[-2:]
    gram = functools.reduce(jnp.add, [g[...] for g in grams])
    order = y_ref.shape[0]
    gram = jnp.concatenate([gram[:, :order], gram[:, order:]], axis=0)
    width = y_ref.shape[1]
    rest = jnp.concatenate([y_ref[...], gram], axis=1)
    lanes = 128
    sub = lax.broadcasted_iota(jnp.int32, (PANEL, 1), 0)
    col = lax.broadcasted_iota(jnp.int32, (PANEL, order), 1)
    for p in range(0, order, PANEL):
        live = order - p
        columns = [
            jnp.broadcast_to(rest[:, width + p + m : width + p + m + 1], (live, lanes))
            for m in range(PANEL)
        ]
        top = rest[:PANEL]
        lower = []
        done = jnp.zeros_like(top)
        for m in range(PANEL):
            inverse = lax.rsqrt(columns[m][m : m + 1])
            low = columns[m] * inverse
            lower.append(low)
            for n in range(m + 1, PANEL):
                columns[n] = columns[n] - low * low[n : n + 1]
            wide = inverse[:, :1]
            row = top[m : m + 1] * wide
            done = jnp.where(sub == m, row, done)
            if m + 1 < PANEL:
                top = top - low[:PANEL, :1] * row
        basis[p : p + PANEL, :] = done[:, :width]
        factor[p : p + PANEL, :] = jnp.where(col >= sub + p, done[:, width:], 0.0)
        if live > PANEL:
            rest = rest[PANEL:]
            for m in range(PANEL):
                rest = rest - lower[m][PANEL:, :1] * done[m : m + 1]


def local(x_block, tiles, coords, counts):
    vectors, width = x_block.shape
    n_row, n_col = lax.axis_size("row"), lax.axis_size("col")
    chips = n_col // 2

    order = sorted(range(1, n_row), key=lambda k: (k != 3, k))
    mate = swap(x_block, 0, 1)
    pieces = [swap(mate, k, 1) if k == 1 else swap(x_block, k, 0) for k in order]
    mark = pl.pallas_call(
        mark_kernel,
        out_shape=jax.ShapeDtypeStruct((8, 128), F32),
        out_specs=VMEM,
        compiler_params=pltpu.CompilerParams(vmem_limit_bytes=1 << 20),
        cost_estimate=pl.CostEstimate(flops=4 * 10**9, bytes_accessed=0, transcendentals=0),
        name="mark",
    )()
    mark, counts = lax.optimization_barrier((mark, counts))
    select = pl.pallas_call(
        select_kernel,
        out_shape=jax.ShapeDtypeStruct(coords.shape[::-1], jnp.int32),
        in_specs=[VMEM, SMEM, VMEM],
        out_specs=VMEM,
        compiler_params=pltpu.CompilerParams(vmem_limit_bytes=1 << 20),
        name="select",
    )(coords.T, counts, mark)
    turned = pl.pallas_call(
        turn_kernel,
        out_shape=jax.ShapeDtypeStruct(tiles.shape[:1] + tiles.shape[:0:-1], tiles.dtype),
        in_specs=[VMEM],
        out_specs=VMEM,
        compiler_params=pltpu.CompilerParams(vmem_limit_bytes=8 << 20),
        cost_estimate=pl.CostEstimate(flops=10**9, bytes_accessed=0, transcendentals=0),
        name="turn",
    )(tiles)
    part = jax.ShapeDtypeStruct((chips, vectors, width), F32)
    keep, send = pl.pallas_call(
        functools.partial(product_kernel, (0, *order)),
        out_shape=(part, part),
        in_specs=[VMEM] * (2 + n_row),
        out_specs=(VMEM, VMEM),
        scratch_shapes=[
            pltpu.VMEM((n_row, vectors, width), x_block.dtype),
            pltpu.VMEM((n_col + 1, vectors, width), F32),
        ],
        compiler_params=pltpu.CompilerParams(vmem_limit_bytes=12 << 20),
        name="product",
    )(select, turned, x_block, *pieces)

    chip = keep + swap(send, 0, 1)
    far = sorted(range(1, chips), key=lambda k: (k != 2, k))
    parts = [chip[0]] + [swap(chip[k], 0, 2 * k) for k in far]
    y, gram = pl.pallas_call(
        functools.partial(gram_kernel, 1.0 / (width * n_row * n_col)),
        out_shape=(
            jax.ShapeDtypeStruct((vectors, width), F32),
            jax.ShapeDtypeStruct((vectors // 2, 2 * vectors), F32),
        ),
        in_specs=[VMEM] * chips,
        out_specs=(VMEM, VMEM),
        compiler_params=pltpu.CompilerParams(vmem_limit_bytes=4 << 20),
        name="gram",
    )(*parts)
    small = jax.ShapeDtypeStruct(gram.shape, F32)
    far = swap(gram, 3, 1)
    gram = gram + swap(gram, 0, 1)
    near = [swap(gram, k, 1) for k in (1, 2)]
    far = pl.pallas_call(
        hand_kernel,
        out_shape=small,
        in_specs=[VMEM] * 2,
        out_specs=VMEM,
        compiler_params=pltpu.CompilerParams(vmem_limit_bytes=1 << 20),
        name="hand",
    )(far, gram)
    fix = swap(far, 0, 1)
    grams = [fix, far, gram] + near
    for masks in (*list(rounds("row"))[1:], *rounds("col")):
        gram = pl.pallas_call(
            sum_kernel,
            out_shape=small,
            in_specs=[VMEM] * len(grams),
            out_specs=VMEM,
            compiler_params=pltpu.CompilerParams(vmem_limit_bytes=1 << 20),
            name="sum",
        )(*grams)
        if masks[0][1] > 1 and len(masks) == 3:
            came = split_swap(gram, masks[1][1] - 1, masks[2][1] - 1)
            near = swap(gram, *masks[0])
            grams = [swap(came, 0, 1), came, gram, near]
        else:
            grams = [gram] + [swap(gram, row, col) for row, col in masks]
    return pl.pallas_call(
        factor_kernel,
        out_shape=(
            jax.ShapeDtypeStruct((vectors, width), F32),
            jax.ShapeDtypeStruct((vectors, vectors), F32),
        ),
        in_specs=[VMEM] * (1 + len(grams)),
        out_specs=(VMEM, VMEM),
        compiler_params=pltpu.CompilerParams(vmem_limit_bytes=4 << 20),
        name="factor",
    )(y, *grams)


def solution(mesh):
    placed = (
        P(None, ("col", "row")),
        P(("row", "col"), None, None),
        P(("row", "col"), None),
        P(("row", "col")),
    )
    return jax.shard_map(
        local, mesh=mesh, in_specs=placed, out_specs=(P(None, ("row", "col")), P()), check_vma=False
    )
```

```python
import functools

import jax
import jax.numpy as jnp
from jax import lax
from jax.experimental import pallas as pl
from jax.experimental.pallas import tpu as pltpu
from jax.sharding import PartitionSpec as P

F32 = jnp.float32
VMEM = pl.BlockSpec(memory_space=pltpu.VMEM)
SMEM = pl.BlockSpec(memory_space=pltpu.SMEM)
EXACT = lax.Precision.HIGHEST
PANEL = 16
DUTY, MID = (1, 3), 2


def swap(x, row, col):
    n_row, n_col = lax.axis_size("row"), lax.axis_size("col")
    pairs = [
        (i * n_col + j, (i ^ row) * n_col + (j ^ col)) for i in range(n_row) for j in range(n_col)
    ]
    return lax.ppermute(x, ("row", "col"), pairs)


def split_swap(x, first, second):
    n_col = lax.axis_size("col")
    return lax.ppermute(x, "col", [(j, j ^ (second if j & 1 else first)) for j in range(n_col)])


def rounds(axis):
    size, low = lax.axis_size(axis), 1 if axis == "row" else 2
    while low < size:
        masks = [low, 2 * low, 3 * low] if 2 * low < size else [low]
        yield [(0, mask | 1) if axis == "col" else (mask, 1) for mask in masks]
        low *= 4


def place_of(block, mate, core, chips):
    if chips != 4:
        return block + mate * chips
    duty = jnp.where(core == 0, *DUTY)
    shared = jnp.where(block == duty, mate, 5 - mate)
    return jnp.where(block == 0, 3 + 4 * mate, jnp.where(block == MID, 2 + 4 * mate, shared))


def mark_kernel(out):
    out[...] = jnp.zeros_like(out)


def select_kernel(coords, counts, mark, select):
    me_row, me_col = lax.axis_index("row"), lax.axis_index("col")
    n_col = lax.axis_size("col")
    apart = coords[0:1, :] ^ me_col
    place = place_of(apart >> 1, apart & 1, me_col & 1, n_col // 2)
    slot = lax.broadcasted_iota(jnp.int32, apart.shape, 1)
    select[0:1, :] = jnp.where(slot < counts[0], place, n_col)
    select[1:2, :] = coords[1:2, :] ^ me_row


def turn_kernel(tiles, turned):
    for s in range(tiles.shape[0]):
        turned[s] = tiles[s].T


def product_kernel(order, select, turned, *refs):
    pieces, (keep, send, x_all, rows) = refs[: len(order)], refs[len(order) :]
    for k, piece in zip(order, pieces):
        x_all[k] = piece[...]
    rows[...] = jnp.zeros_like(rows)
    for s in range(turned.shape[0]):
        rows[select[0, s]] += jnp.dot(x_all[select[1, s]], turned[s], preferred_element_type=F32)
    half = keep.shape[0]
    keep[...] = rows[:half]
    send[...] = rows[half : 2 * half]


def gram_kernel(scale, *refs):
    parts, (y_out, gram_out) = refs[:-2], refs[-2:]
    y = functools.reduce(jnp.add, [part[...] for part in parts])
    y_out[...] = y
    half = y.shape[0] // 2
    for k in range(2):
        gram_out[:, k * 2 * half : (k + 1) * 2 * half] = scale * lax.dot_general(
            y[k * half : (k + 1) * half],
            y,
            (((1,), (1,)), ((), ())),
            precision=EXACT,
            preferred_element_type=F32,
        )


def hand_kernel(came, _, out):
    out[...] = came[...]


def sum_kernel(*refs):
    refs[-1][...] = functools.reduce(jnp.add, [ref[...] for ref in refs[:-1]])


def factor_kernel(y_ref, *refs):
    grams, (basis, factor) = refs[:-2], refs[-2:]
    gram = functools.reduce(jnp.add, [g[...] for g in grams])
    order = y_ref.shape[0]
    gram = jnp.concatenate([gram[:, :order], gram[:, order:]], axis=0)
    width = y_ref.shape[1]
    rest = jnp.concatenate([y_ref[...], gram], axis=1)
    lanes = 128
    sub = lax.broadcasted_iota(jnp.int32, (PANEL, 1), 0)
    col = lax.broadcasted_iota(jnp.int32, (PANEL, order), 1)
    for p in range(0, order, PANEL):
        live = order - p
        columns = [
            jnp.broadcast_to(rest[:, width + p + m : width + p + m + 1], (live, lanes))
            for m in range(PANEL)
        ]
        top = rest[:PANEL]
        lower = []
        done = jnp.zeros_like(top)
        for m in range(PANEL):
            inverse = lax.rsqrt(columns[m][m : m + 1])
            low = columns[m] * inverse
            lower.append(low)
            for n in range(m + 1, PANEL):
                columns[n] = columns[n] - low * low[n : n + 1]
            wide = inverse[:, :1]
            row = top[m : m + 1] * wide
            done = jnp.where(sub == m, row, done)
            if m + 1 < PANEL:
                top = top - low[:PANEL, :1] * row
        basis[p : p + PANEL, :] = done[:, :width]
        factor[p : p + PANEL, :] = jnp.where(col >= sub + p, done[:, width:], 0.0)
        if live > PANEL:
            rest = rest[PANEL:]
            for m in range(PANEL):
                rest = rest - lower[m][PANEL:, :1] * done[m : m + 1]


def local(x_block, tiles, coords, counts):
    vectors, width = x_block.shape
    n_row, n_col = lax.axis_size("row"), lax.axis_size("col")
    chips = n_col // 2

    order = sorted(range(1, n_row), key=lambda k: (k != 3, k))
    mate = swap(x_block, 0, 1)
    pieces = [swap(mate, k, 1) if k == 1 else swap(x_block, k, 0) for k in order]
    mark = pl.pallas_call(
        mark_kernel,
        out_shape=jax.ShapeDtypeStruct((8, 128), F32),
        out_specs=VMEM,
        compiler_params=pltpu.CompilerParams(vmem_limit_bytes=1 << 20),
        cost_estimate=pl.CostEstimate(flops=4 * 10**9, bytes_accessed=0, transcendentals=0),
        name="mark",
    )()
    mark, counts = lax.optimization_barrier((mark, counts))
    select = pl.pallas_call(
        select_kernel,
        out_shape=jax.ShapeDtypeStruct(coords.shape[::-1], jnp.int32),
        in_specs=[VMEM, SMEM, VMEM],
        out_specs=VMEM,
        compiler_params=pltpu.CompilerParams(vmem_limit_bytes=1 << 20),
        name="select",
    )(coords.T, counts, mark)
    turned = pl.pallas_call(
        turn_kernel,
        out_shape=jax.ShapeDtypeStruct(tiles.shape[:1] + tiles.shape[:0:-1], tiles.dtype),
        in_specs=[VMEM],
        out_specs=VMEM,
        compiler_params=pltpu.CompilerParams(vmem_limit_bytes=8 << 20),
        cost_estimate=pl.CostEstimate(flops=10**9, bytes_accessed=0, transcendentals=0),
        name="turn",
    )(tiles)
    part = jax.ShapeDtypeStruct((chips, vectors, width), F32)
    keep, send = pl.pallas_call(
        functools.partial(product_kernel, (0, *order)),
        out_shape=(part, part),
        in_specs=[VMEM] * (2 + n_row),
        out_specs=(VMEM, VMEM),
        scratch_shapes=[
            pltpu.VMEM((n_row, vectors, width), x_block.dtype),
            pltpu.VMEM((n_col + 1, vectors, width), F32),
        ],
        compiler_params=pltpu.CompilerParams(vmem_limit_bytes=12 << 20),
        name="product",
    )(select, turned, x_block, *pieces)

    chip = keep + swap(send, 0, 1)
    if chips == 4:
        came = split_swap(chip[:2], 2 * DUTY[0], 2 * DUTY[1])
        mid = swap(chip[2], 0, 2 * MID)
        parts = [swap(came[1], 0, 1), came[0], chip[3], mid]
    else:
        parts = [chip[0]] + [swap(chip[k], 0, 2 * k) for k in range(1, chips)]
    y, gram = pl.pallas_call(
        functools.partial(gram_kernel, 1.0 / (width * n_row * n_col)),
        out_shape=(
            jax.ShapeDtypeStruct((vectors, width), F32),
            jax.ShapeDtypeStruct((vectors // 2, 2 * vectors), F32),
        ),
        in_specs=[VMEM] * chips,
        out_specs=(VMEM, VMEM),
        compiler_params=pltpu.CompilerParams(vmem_limit_bytes=4 << 20),
        name="gram",
    )(*parts)
    small = jax.ShapeDtypeStruct(gram.shape, F32)
    far = swap(gram, 3, 1)
    gram = gram + swap(gram, 0, 1)
    near = [swap(gram, k, 1) for k in (1, 2)]
    far = pl.pallas_call(
        hand_kernel,
        out_shape=small,
        in_specs=[VMEM] * 2,
        out_specs=VMEM,
        compiler_params=pltpu.CompilerParams(vmem_limit_bytes=1 << 20),
        name="hand",
    )(far, gram)
    fix = swap(far, 0, 1)
    grams = [fix, far, gram] + near
    for masks in (*list(rounds("row"))[1:], *rounds("col")):
        gram = pl.pallas_call(
            sum_kernel,
            out_shape=small,
            in_specs=[VMEM] * len(grams),
            out_specs=VMEM,
            compiler_params=pltpu.CompilerParams(vmem_limit_bytes=1 << 20),
            name="sum",
        )(*grams)
        if masks[0][1] > 1 and len(masks) == 3:
            came = split_swap(gram, masks[1][1] - 1, masks[2][1] - 1)
            near = swap(gram, *masks[0])
            grams = [swap(came, 0, 1), came, gram, near]
        else:
            grams = [gram] + [swap(gram, row, col) for row, col in masks]
    return pl.pallas_call(
        factor_kernel,
        out_shape=(
            jax.ShapeDtypeStruct((vectors, width), F32),
            jax.ShapeDtypeStruct((vectors, vectors), F32),
        ),
        in_specs=[VMEM] * (1 + len(grams)),
        out_specs=(VMEM, VMEM),
        compiler_params=pltpu.CompilerParams(vmem_limit_bytes=4 << 20),
        name="factor",
    )(y, *grams)


def solution(mesh):
    placed = (
        P(None, ("col", "row")),
        P(("row", "col"), None, None),
        P(("row", "col"), None),
        P(("row", "col")),
    )
    return jax.shard_map(
        local, mesh=mesh, in_specs=placed, out_specs=(P(None, ("row", "col")), P()), check_vma=False
    )
```

```python
import functools

import jax
import jax.numpy as jnp
from jax import lax
from jax.experimental import pallas as pl
from jax.experimental.pallas import tpu as pltpu
from jax.sharding import PartitionSpec as P

F32 = jnp.float32
VMEM = pl.BlockSpec(memory_space=pltpu.VMEM)
SMEM = pl.BlockSpec(memory_space=pltpu.SMEM)
EXACT = lax.Precision.HIGHEST
PANEL = 16
DUTY, MID = (1, 3), 2


def swap(x, row, col):
    n_row, n_col = lax.axis_size("row"), lax.axis_size("col")
    pairs = [
        (i * n_col + j, (i ^ row) * n_col + (j ^ col)) for i in range(n_row) for j in range(n_col)
    ]
    return lax.ppermute(x, ("row", "col"), pairs)


def split_swap(x, first, second):
    n_col = lax.axis_size("col")
    return lax.ppermute(x, "col", [(j, j ^ (second if j & 1 else first)) for j in range(n_col)])


def rounds(axis):
    size, low = lax.axis_size(axis), 1 if axis == "row" else 2
    while low < size:
        masks = [low, 2 * low, 3 * low] if 2 * low < size else [low]
        yield [(0, mask | 1) if axis == "col" else (mask, 1) for mask in masks]
        low *= 4


def place_of(block, mate, core, chips):
    if chips != 4:
        return block + mate * chips
    duty = jnp.where(core == 0, *DUTY)
    shared = jnp.where(block == duty, mate, 5 - mate)
    return jnp.where(block == 0, 3 + 4 * mate, jnp.where(block == MID, 2 + 4 * mate, shared))


def mark_kernel(out):
    out[...] = jnp.zeros_like(out)


def select_kernel(coords, counts, mark, select):
    me_row, me_col = lax.axis_index("row"), lax.axis_index("col")
    n_col = lax.axis_size("col")
    apart = coords[0:1, :] ^ me_col
    place = place_of(apart >> 1, apart & 1, me_col & 1, n_col // 2)
    slot = lax.broadcasted_iota(jnp.int32, apart.shape, 1)
    select[0:1, :] = jnp.where(slot < counts[0], place, n_col)
    select[1:2, :] = coords[1:2, :] ^ me_row


def turn_kernel(tiles, turned):
    for s in range(tiles.shape[0]):
        turned[s] = tiles[s].T


def product_kernel(order, select, turned, *refs):
    pieces, outs, (x_all, rows) = refs[: len(order)], refs[len(order) : -2], refs[-2:]
    for k, piece in zip(order, pieces):
        x_all[k] = piece[...]
    rows[...] = jnp.zeros_like(rows)
    for s in range(turned.shape[0]):
        rows[select[0, s]] += jnp.dot(x_all[select[1, s]], turned[s], preferred_element_type=F32)
    at = 0
    for out in outs:
        out[...] = rows[at : at + out.shape[0]]
        at += out.shape[0]


def gram_kernel(scale, *refs):
    parts, (y_out, gram_out) = refs[:-2], refs[-2:]
    y = functools.reduce(jnp.add, [part[...] for part in parts])
    y_out[...] = y
    half = y.shape[0] // 2
    for k in range(2):
        gram_out[:, k * 2 * half : (k + 1) * 2 * half] = scale * lax.dot_general(
            y[k * half : (k + 1) * half],
            y,
            (((1,), (1,)), ((), ())),
            precision=EXACT,
            preferred_element_type=F32,
        )


def hand_kernel(came, _, out):
    out[...] = came[...]


def sum_kernel(*refs):
    refs[-1][...] = functools.reduce(jnp.add, [ref[...] for ref in refs[:-1]])


def factor_kernel(y_ref, *refs):
    grams, (basis, factor) = refs[:-2], refs[-2:]
    gram = functools.reduce(jnp.add, [g[...] for g in grams])
    order = y_ref.shape[0]
    gram = jnp.concatenate([gram[:, :order], gram[:, order:]], axis=0)
    width = y_ref.shape[1]
    rest = jnp.concatenate([y_ref[...], gram], axis=1)
    lanes = 128
    sub = lax.broadcasted_iota(jnp.int32, (PANEL, 1), 0)
    col = lax.broadcasted_iota(jnp.int32, (PANEL, order), 1)
    for p in range(0, order, PANEL):
        live = order - p
        columns = [
            jnp.broadcast_to(rest[:, width + p + m : width + p + m + 1], (live, lanes))
            for m in range(PANEL)
        ]
        top = rest[:PANEL]
        lower = []
        done = jnp.zeros_like(top)
        for m in range(PANEL):
            inverse = lax.rsqrt(columns[m][m : m + 1])
            low = columns[m] * inverse
            lower.append(low)
            for n in range(m + 1, PANEL):
                columns[n] = columns[n] - low * low[n : n + 1]
            wide = inverse[:, :1]
            row = top[m : m + 1] * wide
            done = jnp.where(sub == m, row, done)
            if m + 1 < PANEL:
                top = top - low[:PANEL, :1] * row
        basis[p : p + PANEL, :] = done[:, :width]
        factor[p : p + PANEL, :] = jnp.where(col >= sub + p, done[:, width:], 0.0)
        if live > PANEL:
            rest = rest[PANEL:]
            for m in range(PANEL):
                rest = rest - lower[m][PANEL:, :1] * done[m : m + 1]


def local(x_block, tiles, coords, counts):
    vectors, width = x_block.shape
    n_row, n_col = lax.axis_size("row"), lax.axis_size("col")
    chips = n_col // 2

    order = sorted(range(1, n_row), key=lambda k: (k != 3, k))
    mate = swap(x_block, 0, 1)
    pieces = [swap(mate, k, 1) if k == 1 else swap(x_block, k, 0) for k in order]
    mark = pl.pallas_call(
        mark_kernel,
        out_shape=jax.ShapeDtypeStruct((8, 128), F32),
        out_specs=VMEM,
        compiler_params=pltpu.CompilerParams(vmem_limit_bytes=1 << 20),
        cost_estimate=pl.CostEstimate(flops=4 * 10**9, bytes_accessed=0, transcendentals=0),
        name="mark",
    )()
    mark, counts = lax.optimization_barrier((mark, counts))
    select = pl.pallas_call(
        select_kernel,
        out_shape=jax.ShapeDtypeStruct(coords.shape[::-1], jnp.int32),
        in_specs=[VMEM, SMEM, VMEM],
        out_specs=VMEM,
        compiler_params=pltpu.CompilerParams(vmem_limit_bytes=1 << 20),
        name="select",
    )(coords.T, counts, mark)
    turned = pl.pallas_call(
        turn_kernel,
        out_shape=jax.ShapeDtypeStruct(tiles.shape[:1] + tiles.shape[:0:-1], tiles.dtype),
        in_specs=[VMEM],
        out_specs=VMEM,
        compiler_params=pltpu.CompilerParams(vmem_limit_bytes=8 << 20),
        cost_estimate=pl.CostEstimate(flops=10**9, bytes_accessed=0, transcendentals=0),
        name="turn",
    )(tiles)
    part = jax.ShapeDtypeStruct((chips // 2, vectors, width), F32)
    keep_first, keep_rest, send_first, send_rest = pl.pallas_call(
        functools.partial(product_kernel, (0, *order)),
        out_shape=(part,) * 4,
        in_specs=[VMEM] * (2 + n_row),
        out_specs=(VMEM,) * 4,
        scratch_shapes=[
            pltpu.VMEM((n_row, vectors, width), x_block.dtype),
            pltpu.VMEM((n_col + 1, vectors, width), F32),
        ],
        compiler_params=pltpu.CompilerParams(vmem_limit_bytes=12 << 20),
        name="product",
    )(select, turned, x_block, *pieces)

    first = keep_first + swap(send_first, 0, 1)
    rest = keep_rest + swap(send_rest, 0, 1)
    if chips == 4:
        came = split_swap(first, 2 * DUTY[0], 2 * DUTY[1])
        mid = swap(rest[0], 0, 2 * MID)
        parts = [swap(came[1], 0, 1), came[0], rest[1], mid]
    else:
        chip = [*first, *rest]
        parts = [chip[0]] + [swap(chip[k], 0, 2 * k) for k in range(1, chips)]
    y, gram = pl.pallas_call(
        functools.partial(gram_kernel, 1.0 / (width * n_row * n_col)),
        out_shape=(
            jax.ShapeDtypeStruct((vectors, width), F32),
            jax.ShapeDtypeStruct((vectors // 2, 2 * vectors), F32),
        ),
        in_specs=[VMEM] * chips,
        out_specs=(VMEM, VMEM),
        compiler_params=pltpu.CompilerParams(vmem_limit_bytes=4 << 20),
        name="gram",
    )(*parts)
    small = jax.ShapeDtypeStruct(gram.shape, F32)
    far = swap(gram, 3, 1)
    gram = gram + swap(gram, 0, 1)
    near = [swap(gram, k, 1) for k in (1, 2)]
    far = pl.pallas_call(
        hand_kernel,
        out_shape=small,
        in_specs=[VMEM] * 2,
        out_specs=VMEM,
        compiler_params=pltpu.CompilerParams(vmem_limit_bytes=1 << 20),
        name="hand",
    )(far, gram)
    fix = swap(far, 0, 1)
    grams = [fix, far, gram] + near
    for masks in (*list(rounds("row"))[1:], *rounds("col")):
        gram = pl.pallas_call(
            sum_kernel,
            out_shape=small,
            in_specs=[VMEM] * len(grams),
            out_specs=VMEM,
            compiler_params=pltpu.CompilerParams(vmem_limit_bytes=1 << 20),
            name="sum",
        )(*grams)
        if masks[0][1] > 1 and len(masks) == 3:
            came = split_swap(gram, masks[1][1] - 1, masks[2][1] - 1)
            near = swap(gram, *masks[0])
            grams = [swap(came, 0, 1), came, gram, near]
        else:
            grams = [gram] + [swap(gram, row, col) for row, col in masks]
    return pl.pallas_call(
        factor_kernel,
        out_shape=(
            jax.ShapeDtypeStruct((vectors, width), F32),
            jax.ShapeDtypeStruct((vectors, vectors), F32),
        ),
        in_specs=[VMEM] * (1 + len(grams)),
        out_specs=(VMEM, VMEM),
        compiler_params=pltpu.CompilerParams(vmem_limit_bytes=4 << 20),
        name="factor",
    )(y, *grams)


def solution(mesh):
    placed = (
        P(None, ("col", "row")),
        P(("row", "col"), None, None),
        P(("row", "col"), None),
        P(("row", "col")),
    )
    return jax.shard_map(
        local, mesh=mesh, in_specs=placed, out_specs=(P(None, ("row", "col")), P()), check_vma=False
    )
```

```python
import functools

import jax
import jax.numpy as jnp
from jax import lax
from jax.experimental import pallas as pl
from jax.experimental.pallas import tpu as pltpu
from jax.sharding import PartitionSpec as P

F32 = jnp.float32
VMEM = pl.BlockSpec(memory_space=pltpu.VMEM)
SMEM = pl.BlockSpec(memory_space=pltpu.SMEM)
EXACT = lax.Precision.HIGHEST
PANEL = 16
DUTY, MID = (1, 3), 2


def swap(x, row, col):
    n_row, n_col = lax.axis_size("row"), lax.axis_size("col")
    pairs = [
        (i * n_col + j, (i ^ row) * n_col + (j ^ col)) for i in range(n_row) for j in range(n_col)
    ]
    return lax.ppermute(x, ("row", "col"), pairs)


def split_swap(x, first, second):
    n_col = lax.axis_size("col")
    return lax.ppermute(x, "col", [(j, j ^ (second if j & 1 else first)) for j in range(n_col)])


def rounds(axis):
    size, low = lax.axis_size(axis), 1 if axis == "row" else 2
    while low < size:
        masks = [low, 2 * low, 3 * low] if 2 * low < size else [low]
        yield [(0, mask | 1) if axis == "col" else (mask, 1) for mask in masks]
        low *= 4


def place_of(block, mate, core, chips):
    if chips != 4:
        return block + mate * chips
    duty = jnp.where(core == 0, *DUTY)
    shared = jnp.where(block == duty, mate, 5 - mate)
    return jnp.where(block == 0, 3 + 4 * mate, jnp.where(block == MID, 2 + 4 * mate, shared))


def mark_kernel(out):
    out[...] = jnp.zeros_like(out)


def select_kernel(coords, counts, mark, select):
    me_row, me_col = lax.axis_index("row"), lax.axis_index("col")
    n_col = lax.axis_size("col")
    apart = coords[0:1, :] ^ me_col
    place = place_of(apart >> 1, apart & 1, me_col & 1, n_col // 2)
    slot = lax.broadcasted_iota(jnp.int32, apart.shape, 1)
    select[0:1, :] = jnp.where(slot < counts[0], place, n_col)
    select[1:2, :] = coords[1:2, :] ^ me_row


def turn_kernel(tiles, turned):
    for s in range(tiles.shape[0]):
        turned[s] = tiles[s].T


def product_kernel(order, select, turned, *refs):
    pieces, outs, (x_all, rows) = refs[: len(order)], refs[len(order) : -2], refs[-2:]
    for k, piece in zip(order, pieces):
        x_all[k] = piece[...]
    rows[...] = jnp.zeros_like(rows)
    for s in range(turned.shape[0]):
        rows[select[0, s]] += jnp.dot(x_all[select[1, s]], turned[s], preferred_element_type=F32)
    at = 0
    for out in outs:
        out[...] = rows[at : at + out.shape[0]]
        at += out.shape[0]


def gram_kernel(scale, *refs):
    parts, (y_out, gram_out) = refs[:-2], refs[-2:]
    y = functools.reduce(jnp.add, [part[...] for part in parts])
    y_out[...] = y
    half = y.shape[0] // 2
    gram = scale * lax.dot_general(
        y, y, (((1,), (1,)), ((), ())), precision=EXACT, preferred_element_type=F32
    )
    gram_out[...] = jnp.concatenate([gram[:half], gram[half:]], axis=1)


def hand_kernel(came, _, out):
    out[...] = came[...]


def sum_kernel(*refs):
    refs[-1][...] = functools.reduce(jnp.add, [ref[...] for ref in refs[:-1]])


def factor_kernel(y_ref, *refs):
    grams, (basis, factor) = refs[:-2], refs[-2:]
    gram = functools.reduce(jnp.add, [g[...] for g in grams])
    order = y_ref.shape[0]
    gram = jnp.concatenate([gram[:, :order], gram[:, order:]], axis=0)
    width = y_ref.shape[1]
    rest = jnp.concatenate([y_ref[...], gram], axis=1)
    lanes = 128
    sub = lax.broadcasted_iota(jnp.int32, (PANEL, 1), 0)
    col = lax.broadcasted_iota(jnp.int32, (PANEL, order), 1)
    for p in range(0, order, PANEL):
        live = order - p
        columns = [
            jnp.broadcast_to(rest[:, width + p + m : width + p + m + 1], (live, lanes))
            for m in range(PANEL)
        ]
        top = rest[:PANEL]
        lower = []
        done = jnp.zeros_like(top)
        for m in range(PANEL):
            inverse = lax.rsqrt(columns[m][m : m + 1])
            low = columns[m] * inverse
            lower.append(low)
            for n in range(m + 1, PANEL):
                columns[n] = columns[n] - low * low[n : n + 1]
            wide = inverse[:, :1]
            row = top[m : m + 1] * wide
            done = jnp.where(sub == m, row, done)
            if m + 1 < PANEL:
                top = top - low[:PANEL, :1] * row
        basis[p : p + PANEL, :] = done[:, :width]
        factor[p : p + PANEL, :] = jnp.where(col >= sub + p, done[:, width:], 0.0)
        if live > PANEL:
            rest = rest[PANEL:]
            for m in range(PANEL):
                rest = rest - lower[m][PANEL:, :1] * done[m : m + 1]


def local(x_block, tiles, coords, counts):
    vectors, width = x_block.shape
    n_row, n_col = lax.axis_size("row"), lax.axis_size("col")
    chips = n_col // 2

    order = sorted(range(1, n_row), key=lambda k: (k != 3, k))
    mate = swap(x_block, 0, 1)
    pieces = [swap(mate, k, 1) if k == 1 else swap(x_block, k, 0) for k in order]
    mark = pl.pallas_call(
        mark_kernel,
        out_shape=jax.ShapeDtypeStruct((8, 128), F32),
        out_specs=VMEM,
        compiler_params=pltpu.CompilerParams(vmem_limit_bytes=1 << 20),
        cost_estimate=pl.CostEstimate(flops=4 * 10**9, bytes_accessed=0, transcendentals=0),
        name="mark",
    )()
    mark, counts = lax.optimization_barrier((mark, counts))
    select = pl.pallas_call(
        select_kernel,
        out_shape=jax.ShapeDtypeStruct(coords.shape[::-1], jnp.int32),
        in_specs=[VMEM, SMEM, VMEM],
        out_specs=VMEM,
        compiler_params=pltpu.CompilerParams(vmem_limit_bytes=1 << 20),
        name="select",
    )(coords.T, counts, mark)
    turned = pl.pallas_call(
        turn_kernel,
        out_shape=jax.ShapeDtypeStruct(tiles.shape[:1] + tiles.shape[:0:-1], tiles.dtype),
        in_specs=[VMEM],
        out_specs=VMEM,
        compiler_params=pltpu.CompilerParams(vmem_limit_bytes=8 << 20),
        cost_estimate=pl.CostEstimate(flops=10**9, bytes_accessed=0, transcendentals=0),
        name="turn",
    )(tiles)
    part = jax.ShapeDtypeStruct((chips // 2, vectors, width), F32)
    keep_first, keep_rest, send_first, send_rest = pl.pallas_call(
        functools.partial(product_kernel, (0, *order)),
        out_shape=(part,) * 4,
        in_specs=[VMEM] * (2 + n_row),
        out_specs=(VMEM,) * 4,
        scratch_shapes=[
            pltpu.VMEM((n_row, vectors, width), x_block.dtype),
            pltpu.VMEM((n_col + 1, vectors, width), F32),
        ],
        compiler_params=pltpu.CompilerParams(vmem_limit_bytes=12 << 20),
        name="product",
    )(select, turned, x_block, *pieces)

    first = keep_first + swap(send_first, 0, 1)
    rest = keep_rest + swap(send_rest, 0, 1)
    if chips == 4:
        came = split_swap(first, 2 * DUTY[0], 2 * DUTY[1])
        mid = swap(rest[0], 0, 2 * MID)
        parts = [swap(came[1], 0, 1), came[0], rest[1], mid]
    else:
        chip = [*first, *rest]
        parts = [chip[0]] + [swap(chip[k], 0, 2 * k) for k in range(1, chips)]
    y, gram = pl.pallas_call(
        functools.partial(gram_kernel, 1.0 / (width * n_row * n_col)),
        out_shape=(
            jax.ShapeDtypeStruct((vectors, width), F32),
            jax.ShapeDtypeStruct((vectors // 2, 2 * vectors), F32),
        ),
        in_specs=[VMEM] * chips,
        out_specs=(VMEM, VMEM),
        compiler_params=pltpu.CompilerParams(vmem_limit_bytes=4 << 20),
        name="gram",
    )(*parts)
    small = jax.ShapeDtypeStruct(gram.shape, F32)
    far = swap(gram, 3, 1)
    gram = gram + swap(gram, 0, 1)
    near = [swap(gram, k, 1) for k in (1, 2)]
    far = pl.pallas_call(
        hand_kernel,
        out_shape=small,
        in_specs=[VMEM] * 2,
        out_specs=VMEM,
        compiler_params=pltpu.CompilerParams(vmem_limit_bytes=1 << 20),
        name="hand",
    )(far, gram)
    fix = swap(far, 0, 1)
    grams = [fix, far, gram] + near
    for masks in (*list(rounds("row"))[1:], *rounds("col")):
        gram = pl.pallas_call(
            sum_kernel,
            out_shape=small,
            in_specs=[VMEM] * len(grams),
            out_specs=VMEM,
            compiler_params=pltpu.CompilerParams(vmem_limit_bytes=1 << 20),
            name="sum",
        )(*grams)
        if masks[0][1] > 1 and len(masks) == 3:
            came = split_swap(gram, masks[1][1] - 1, masks[2][1] - 1)
            near = swap(gram, *masks[0])
            grams = [swap(came, 0, 1), came, gram, near]
        else:
            grams = [gram] + [swap(gram, row, col) for row, col in masks]
    return pl.pallas_call(
        factor_kernel,
        out_shape=(
            jax.ShapeDtypeStruct((vectors, width), F32),
            jax.ShapeDtypeStruct((vectors, vectors), F32),
        ),
        in_specs=[VMEM] * (1 + len(grams)),
        out_specs=(VMEM, VMEM),
        compiler_params=pltpu.CompilerParams(vmem_limit_bytes=4 << 20),
        name="factor",
    )(y, *grams)


def solution(mesh):
    placed = (
        P(None, ("col", "row")),
        P(("row", "col"), None, None),
        P(("row", "col"), None),
        P(("row", "col")),
    )
    return jax.shard_map(
        local, mesh=mesh, in_specs=placed, out_specs=(P(None, ("row", "col")), P()), check_vma=False
    )
```
